32 devices in a mesh: segment: 2 (over x), expert: 8 (over z, y), dp: 2 (over core).
Axes of the slice: x: 2, y: 2, z: 4, core: 2. Of those that a mesh axis runs over, the one named last changes fastest.
Arguments:
- entering: bfloat16 [2, 1024, 2560], P('segment', ('expert', 'dp')), may hold values from -0.59765625 to 0.59765625
- fresh: bfloat16 [1, 1024, 2560], P(None, ('expert', 'dp')), may hold values from -0.59765625 to 0.59765625
- w_gate: bfloat16 [2, 16, 2560, 768], P('segment', ('expert', 'dp')), may hold values from -0.125 to 0.125
- w_up: bfloat16 [2, 16, 2560, 768], P('segment', ('expert', 'dp')), may hold values from -0.125 to 0.125
- w_down: bfloat16 [2, 16, 768, 2560], P('segment', ('expert', 'dp')), may hold values from -0.21875 to 0.21875
- router: bfloat16 [2, 2560, 16], P('segment'), may hold values from -0.0625 to 0.0625
- gain: float32 [2, 2560], P('segment'), may hold values from 0.5 to 2
- routes: int32 [2, 2, 1024, 6], P('segment', None, ('expert', 'dp')), may hold values from 0 to 15, all different within a row; in each aligned block of 64 rows (0 to 63, 64 to 127, ..., all dimensions but the last counted through in order) at most 32 rows name the same one
Outputs:
- section_out: bfloat16 [2, 2, 1024, 2560], P('segment', None, ('expert', 'dp'))
The draws below stay inside these ranges and needn't reach their ends.
Inputs may be any that keep to these rules, and one draw needn't show every extreme that they name: `routes`: in every aligned block of 64 rows (the tokens of one device for one section and micro-batch) no expert is named by more than 32 rows, and in some blocks one expert is named by exactly 32 rows; a row names 6 different experts.
All inputs are finite; a program needn't handle non-finite values.
Results may differ from the reference program's by a relative error of at most 0.009.
Values may be sent and summed in bfloat16 or wider, within the bound.
A program may use at most 64 MiB of HBM per device.

```python
import math
import jax
import jax.numpy as jnp
import numpy as np
from jax import lax

D = 2560
HID = 768
TOPK = 6
MICRO = 2
TOK_DEV = 64
LAYERS = 2
EXPERTS = 16
TOKENS = 1024
CAP = 32


def block_scale(key, dims, split, low, largest):
    level, own = 1.0, jax.random.fold_in(key, 6)
    for position, shards_of in split:
        steps = jnp.exp(jax.random.uniform(jax.random.fold_in(own, position), (shards_of,), jnp.float32, low / len(split), largest / len(split)))
        level = level * jnp.repeat(steps, dims[position] // shards_of).reshape([-1 if axis == position else 1 for axis in range(len(dims))])
    return level


def deal_out(stream_key, own, number, rows, number_of, top, bound, slope):
    sequence = jax.random.permutation(stream_key, number_of)
    heavy_load, common = load_shares(number_of, rows * top, bound, slope, True), load_shares(number_of, rows * top, bound, slope, False)
    places = jnp.arange(number_of)

    def named(tallies, turn):
        used = int((tallies > 0).sum())
        fixed = max(1, used // 4)
        shifted = fixed + (places - fixed + turn * (used - fixed)) % max(1, number_of - fixed)
        return jnp.zeros((number_of,), jnp.int32).at[sequence[jnp.where(places < fixed, places, shifted)]].set(jnp.asarray(tallies, jnp.int32))

    tallies = jnp.where(number % 4 == 0, named(heavy_load, number // 4), named(common, number - number // 4 - 1))
    mixed = jax.random.permutation(jax.random.fold_in(own, 3), number_of)
    giver, receiver = mixed[0:number_of // 2 * 2:2], mixed[1:number_of // 2 * 2:2]
    margin = jnp.minimum(tallies[giver] - 1, bound - tallies[receiver]) // 2
    margin = jnp.where((giver == sequence[0]) | (receiver == sequence[0]) | (tallies[receiver] == 0), 0, jnp.maximum(margin, 0))
    shifted = jax.random.randint(jax.random.fold_in(own, 4), (number_of // 2,), 0, 1 << 20) % (margin + 1)
    tallies = tallies.at[giver].add(-shifted).at[receiver].add(shifted)
    labels = jnp.searchsorted(jnp.cumsum(tallies), jnp.arange(rows * top), side="right").astype(jnp.int32)
    grid = labels.reshape(top, rows).T
    grid = grid[jax.random.permutation(jax.random.fold_in(own, 1), rows)]
    turn = jax.random.randint(jax.random.fold_in(own, 2), (rows, 1), 0, top)
    return jnp.take_along_axis(grid, (jnp.arange(top)[None, :] + turn) % top, axis=1)


def load_shares(amount, total, limit, lean, full):
    portions = [(1 << 20) // math.isqrt(rank ** lean) + 1 for rank in range(1, amount + 1)]
    largest = limit if full else min(limit, max(-(-total // amount), total * portions[0] // sum(portions)))
    least = 1 if total - largest >= amount - 1 else 0
    given, spare = [largest] + [least] * (amount - 1), total - largest - least * (amount - 1)
    while spare > 0:
        movable = [i for i in range(1, amount) if given[i] < largest] or [i for i in range(1, amount) if given[i] < limit]
        mass, remaining = sum([portions[i] for i in movable]), spare
        for i in movable:
            extra = min(limit - given[i], max(1, remaining * portions[i] // mass), spare)
            given[i] = given[i] + extra
            spare = spare - extra
    return np.array(given)


def bell_draw(stream_key, shape, spread, reach, shards=(), held_as=jnp.bfloat16):
    factor_of = block_scale(stream_key, shape, shards, -0.22, 0.18) if shards else 1.0
    drawn = jax.random.normal(stream_key, shape, jnp.float32) * spread * factor_of
    return jnp.minimum(jnp.maximum(drawn, -reach), reach).astype(held_as)


def setup_inputs(seed: int = 0) -> dict:
    streams_of = jax.random.split(jax.random.key(seed), 9)
    entering = bell_draw(streams_of[0], (LAYERS, TOKENS, D), 0.1, 0.59765625, ((0, 2), (1, 16)))
    fresh = bell_draw(streams_of[1], (MICRO - 1, TOKENS, D), 0.1, 0.59765625, ((1, 16),))
    w_gate = bell_draw(streams_of[2], (LAYERS, EXPERTS, D, HID), D ** -0.5, 0.125, ((0, 2), (1, 16)))
    w_up = bell_draw(streams_of[3], (LAYERS, EXPERTS, D, HID), D ** -0.5, 0.125, ((0, 2), (1, 16)))
    w_down = bell_draw(streams_of[4], (LAYERS, EXPERTS, HID, D), HID ** -0.5, 0.21875, ((0, 2), (1, 16)))
    router = bell_draw(streams_of[5], (LAYERS, D, EXPERTS), (4 * D) ** -0.5, 0.0625, ((0, 2),))
    gain = jnp.clip(jnp.exp(math.log(2.0) - 1.3862944 * jax.random.uniform(streams_of[6], (LAYERS, D), jnp.float32) ** block_scale(streams_of[6], (LAYERS, D), ((0, 2),), -0.2, 0.2)), 0.5, 2.0)
    routes_keys = jax.random.split(jax.random.fold_in(streams_of[7], 1), LAYERS * MICRO * TOKENS // TOK_DEV)
    routes_turns = jax.random.permutation(jax.random.fold_in(streams_of[7], 3), LAYERS * MICRO * TOKENS // TOK_DEV)
    routes = jax.vmap(lambda own, number: deal_out(jax.random.fold_in(streams_of[7], 2), own, number, TOK_DEV, EXPERTS, TOPK, CAP, 2))(routes_keys, routes_turns).reshape((LAYERS, MICRO, TOKENS, TOPK))
    return dict(entering=entering, fresh=fresh, w_gate=w_gate, w_up=w_up, w_down=w_down, router=router, gain=gain, routes=routes)


def expert_rows(slot_rows, gate_weight, up_weight, down_weight):
    model_width = slot_rows.shape[-1]
    flattened = slot_rows.reshape(-1, model_width)
    gate_out = jnp.dot(flattened, gate_weight, preferred_element_type=jnp.float32)
    upper = jnp.dot(flattened, up_weight, preferred_element_type=jnp.float32)
    hidden = (jax.nn.silu(gate_out) * upper).astype(jnp.bfloat16)
    projected = jnp.dot(hidden, down_weight, preferred_element_type=jnp.float32).astype(jnp.bfloat16)
    return projected.reshape(slot_rows.shape)

def routed_slots(chosen_ids, expert_count):
    onehot = (chosen_ids[:, None] == jnp.arange(expert_count, dtype=jnp.int32)[None, :]).astype(jnp.int32)
    before = jnp.cumsum(onehot, axis=0) - onehot
    return lax.optimization_barrier(jnp.sum(before * onehot, axis=1)).astype(jnp.int32)

def section_all(incoming, gate_weight, up_weight, down_weight, router_layer, gain_layer, chosen_ids):
    device_count = TOKENS // TOK_DEV
    values = incoming.astype(jnp.float32)
    inv_scale = lax.rsqrt(lax.optimization_barrier(jnp.mean(values * values, axis=1, keepdims=True)) + 1e-06)
    normed = (values * inv_scale * gain_layer[None, :]).astype(jnp.bfloat16)
    logits = jnp.dot(normed, router_layer, preferred_element_type=jnp.float32)
    scores = jax.nn.sigmoid(logits)
    chosen = jnp.take_along_axis(scores, chosen_ids, axis=1)
    mixing = chosen / lax.optimization_barrier(jnp.sum(chosen, axis=1, keepdims=True))
    block_ids = chosen_ids.reshape(device_count, TOK_DEV * TOPK).astype(jnp.int32)
    slot_ids = jax.vmap(lambda ids: routed_slots(ids, EXPERTS))(block_ids)
    owners = jnp.broadcast_to((jnp.arange(TOK_DEV * TOPK, dtype=jnp.int32) // TOPK)[None, :], block_ids.shape)
    device_ids = jnp.broadcast_to(jnp.arange(device_count, dtype=jnp.int32)[:, None], block_ids.shape)
    source = jnp.full((device_count, EXPERTS, CAP), TOK_DEV, jnp.int32).at[device_ids, block_ids, slot_ids].set(owners)
    padded = jnp.concatenate([normed.reshape(device_count, TOK_DEV, D), jnp.zeros((device_count, 1, D), jnp.bfloat16)], axis=1)
    outgoing = jax.vmap(lambda table, where_from: table[where_from])(padded, source)
    arranged = jnp.swapaxes(outgoing, 0, 1)
    processed = lax.map(lambda packed: expert_rows(packed[0], packed[1], packed[2], packed[3]), (arranged, gate_weight, up_weight, down_weight))
    landed = processed[block_ids, device_ids, slot_ids].reshape(TOKENS, TOPK, D)
    summed = values + lax.optimization_barrier(jnp.sum(landed.astype(jnp.float32) * mixing[:, :, None], axis=1))
    return summed.astype(jnp.bfloat16)

def reference(entering, fresh, w_gate, w_up, w_down, router, gain, routes):
    outputs_all = []
    previous = None
    for step_index in range(MICRO):
        row_list = []
        for segment_index in range(LAYERS):
            if step_index == 0:
                incoming = entering[segment_index]
            elif segment_index == 0:
                incoming = fresh[step_index - 1]
            else:
                incoming = previous[segment_index - 1]
            row_list.append(section_all(incoming, w_gate[segment_index], w_up[segment_index], w_down[segment_index], router[segment_index], gain[segment_index], routes[segment_index, step_index]))
        previous = row_list
        outputs_all.append(row_list)
    return jnp.stack([jnp.stack([outputs_all[step_index][segment_index] for step_index in range(MICRO)]) for segment_index in range(LAYERS)])
```

```python
import jax
import jax.numpy as jnp
from jax import lax
from jax.sharding import PartitionSpec as P


def shifted(value, axis, steps):
    count = lax.axis_size(axis)
    leading, last = (max(0, -steps), min(count, count - steps))
    return lax.ppermute(value, axis, [(source, source + steps) for source in range(leading, last)])


def expert_rows(slot_rows, gate_weight, up_weight, down_weight):
    model_width = slot_rows.shape[-1]
    flattened = slot_rows.reshape(-1, model_width)
    gate_out = jnp.dot(flattened, gate_weight, preferred_element_type=jnp.float32)
    upper = jnp.dot(flattened, up_weight, preferred_element_type=jnp.float32)
    hidden = (jax.nn.silu(gate_out) * upper).astype(jnp.bfloat16)
    projected = jnp.dot(hidden, down_weight, preferred_element_type=jnp.float32).astype(
        jnp.bfloat16
    )
    return projected.reshape(slot_rows.shape)


def routed_slots(chosen_ids, expert_count):
    onehot = (chosen_ids[:, None] == jnp.arange(expert_count, dtype=jnp.int32)[None, :]).astype(
        jnp.int32
    )
    before = jnp.cumsum(onehot, axis=0) - onehot
    return jnp.sum(before * onehot, axis=1)


def section(incoming, gate_weight, up_weight, down_weight, router_layer, gain_layer, chosen_ids):
    tok_rows, model_width = incoming.shape
    top_count = chosen_ids.shape[1]
    experts = router_layer.shape[1]
    capacity = 4 * tok_rows * top_count // (3 * experts)
    values = incoming.astype(jnp.float32)
    inv_scale = lax.rsqrt(jnp.mean(values * values, axis=1, keepdims=True) + 1e-06)
    normed = (values * inv_scale * gain_layer[None, :]).astype(jnp.bfloat16)
    logits = jnp.dot(normed, router_layer, preferred_element_type=jnp.float32)
    scores = jax.nn.sigmoid(logits)
    chosen = jnp.take_along_axis(scores, chosen_ids, axis=1)
    mixing = chosen / jnp.sum(chosen, axis=1, keepdims=True)
    flat_picks = chosen_ids.reshape(-1)
    slot_ids = routed_slots(flat_picks, experts)
    owners = jnp.arange(tok_rows * top_count, dtype=jnp.int32) // top_count
    source = jnp.full((experts, capacity), tok_rows, jnp.int32).at[flat_picks, slot_ids].set(owners)
    padded = jnp.concatenate([normed, jnp.zeros((1, model_width), jnp.bfloat16)], axis=0)
    outgoing = padded[source]
    processed = expert_rows(
        lax.all_to_all(outgoing, ("expert", "dp"), split_axis=0, concat_axis=0, tiled=True),
        gate_weight,
        up_weight,
        down_weight,
    )
    returned = lax.all_to_all(processed, ("expert", "dp"), split_axis=0, concat_axis=0, tiled=True)
    landed = returned[flat_picks, slot_ids].reshape(tok_rows, top_count, model_width)
    summed = values + jnp.sum(landed.astype(jnp.float32) * mixing[:, :, None], axis=1)
    return summed.astype(jnp.bfloat16)


def mixed_weights(normed, router_layer, chosen_ids):
    experts = router_layer.shape[1]
    logits = jnp.dot(normed, router_layer, preferred_element_type=jnp.float32)
    ids = jnp.arange(experts, dtype=jnp.int32)
    named = jnp.any(chosen_ids[:, :, None] == ids[None, None, :], axis=1)
    scores = jnp.where(named, jax.nn.sigmoid(logits), 0.0)
    return scores / jnp.sum(scores, axis=1, keepdims=True)


def gathered_section(
    incoming, gate_weight, up_weight, down_weight, router_layer, gain_layer, chosen_ids
):
    values = incoming.astype(jnp.float32)
    inv_scale = lax.rsqrt(jnp.mean(values * values, axis=1, keepdims=True) + 1e-06)
    normed = (values * inv_scale * gain_layer[None, :]).astype(jnp.bfloat16)
    mixing = mixed_weights(normed, router_layer, chosen_ids)
    axes = ("expert", "dp")
    tokens = lax.all_gather(normed, axes, axis=0, tiled=True)
    mine = lax.all_to_all(mixing.T, axes, split_axis=0, concat_axis=1, tiled=True)
    gate_out = jnp.dot(tokens, gate_weight, preferred_element_type=jnp.float32)
    upper = jnp.dot(tokens, up_weight, preferred_element_type=jnp.float32)
    hidden = (jax.nn.silu(gate_out) * upper).astype(jnp.bfloat16)
    projected = jnp.dot(hidden, down_weight, preferred_element_type=jnp.float32)
    shares = (projected * mine.reshape(-1, 1)).astype(jnp.bfloat16)
    summed = lax.psum_scatter(shares, axes, scatter_dimension=0, tiled=True)
    return (values + summed.astype(jnp.float32)).astype(jnp.bfloat16)


def shards(entering, fresh, w_gate, w_up, w_down, router, gain, routes):
    segment_id = lax.axis_index("segment")
    tok_rows, top_count = routes.shape[2:]
    capacity = 4 * tok_rows * top_count // (3 * router.shape[2])
    layer = gathered_section if tok_rows <= 2 * capacity else section
    micro_count = routes.shape[1]
    current = entering[0]
    results = []
    for step_index in range(micro_count):
        if step_index > 0:
            arrived = shifted(results[-1], "segment", 1)
            current = jnp.where(segment_id == 0, fresh[step_index - 1], arrived)
        output = layer(
            current,
            w_gate[0, 0],
            w_up[0, 0],
            w_down[0, 0],
            router[0],
            gain[0],
            routes[0, step_index],
        )
        results.append(output)
    return jnp.stack(results)[None]


def solution(mesh):
    in_specs = (
        P("segment", ("expert", "dp"), None),
        P(None, ("expert", "dp"), None),
        P("segment", ("expert", "dp"), None, None),
        P("segment", ("expert", "dp"), None, None),
        P("segment", ("expert", "dp"), None, None),
        P("segment", None, None),
        P("segment", None),
        P("segment", None, ("expert", "dp"), None),
    )
    out_specs = P("segment", None, ("expert", "dp"), None)
    return jax.shard_map(shards, mesh=mesh, in_specs=in_specs, out_specs=out_specs, check_vma=False)
```

```python
import functools

import jax
import jax.numpy as jnp
from jax import lax
from jax.experimental import pallas as pl
from jax.experimental.pallas import tpu as pltpu
from jax.sharding import PartitionSpec as P


def shifted(value, axis, steps):
    count = lax.axis_size(axis)
    leading, last = (max(0, -steps), min(count, count - steps))
    return lax.ppermute(value, axis, [(source, source + steps) for source in range(leading, last)])


def expert_rows(slot_rows, gate_weight, up_weight, down_weight):
    model_width = slot_rows.shape[-1]
    flattened = slot_rows.reshape(-1, model_width)
    gate_out = jnp.dot(flattened, gate_weight, preferred_element_type=jnp.float32)
    upper = jnp.dot(flattened, up_weight, preferred_element_type=jnp.float32)
    hidden = (jax.nn.silu(gate_out) * upper).astype(jnp.bfloat16)
    projected = jnp.dot(hidden, down_weight, preferred_element_type=jnp.float32).astype(
        jnp.bfloat16
    )
    return projected.reshape(slot_rows.shape)


def routed_slots(chosen_ids, expert_count):
    onehot = (chosen_ids[:, None] == jnp.arange(expert_count, dtype=jnp.int32)[None, :]).astype(
        jnp.int32
    )
    before = jnp.cumsum(onehot, axis=0) - onehot
    return jnp.sum(before * onehot, axis=1)


def section(incoming, gate_weight, up_weight, down_weight, router_layer, gain_layer, chosen_ids):
    tok_rows, model_width = incoming.shape
    top_count = chosen_ids.shape[1]
    experts = router_layer.shape[1]
    capacity = 4 * tok_rows * top_count // (3 * experts)
    values = incoming.astype(jnp.float32)
    inv_scale = lax.rsqrt(jnp.mean(values * values, axis=1, keepdims=True) + 1e-06)
    normed = (values * inv_scale * gain_layer[None, :]).astype(jnp.bfloat16)
    logits = jnp.dot(normed, router_layer, preferred_element_type=jnp.float32)
    scores = jax.nn.sigmoid(logits)
    chosen = jnp.take_along_axis(scores, chosen_ids, axis=1)
    mixing = chosen / jnp.sum(chosen, axis=1, keepdims=True)
    flat_picks = chosen_ids.reshape(-1)
    slot_ids = routed_slots(flat_picks, experts)
    owners = jnp.arange(tok_rows * top_count, dtype=jnp.int32) // top_count
    source = jnp.full((experts, capacity), tok_rows, jnp.int32).at[flat_picks, slot_ids].set(owners)
    padded = jnp.concatenate([normed, jnp.zeros((1, model_width), jnp.bfloat16)], axis=0)
    outgoing = padded[source]
    processed = expert_rows(
        lax.all_to_all(outgoing, ("expert", "dp"), split_axis=0, concat_axis=0, tiled=True),
        gate_weight,
        up_weight,
        down_weight,
    )
    returned = lax.all_to_all(processed, ("expert", "dp"), split_axis=0, concat_axis=0, tiled=True)
    landed = returned[flat_picks, slot_ids].reshape(tok_rows, top_count, model_width)
    summed = values + jnp.sum(landed.astype(jnp.float32) * mixing[:, :, None], axis=1)
    return summed.astype(jnp.bfloat16)


def shards(entering, fresh, w_gate, w_up, w_down, router, gain, routes):
    segment_id = lax.axis_index("segment")
    micro_count = routes.shape[1]
    current = entering[0]
    results = []
    for step_index in range(micro_count):
        if step_index > 0:
            arrived = shifted(results[-1], "segment", 1)
            current = jnp.where(segment_id == 0, fresh[step_index - 1], arrived)
        output = section(
            current,
            w_gate[0, 0],
            w_up[0, 0],
            w_down[0, 0],
            router[0],
            gain[0],
            routes[0, step_index],
        )
        results.append(output)
    return jnp.stack(results)[None]


LANES = 128
MESH = pl.DeviceIdType.MESH


def near_first(order, z, nz):
    low, high = z, nz - 1 - z
    paired = 2 * jnp.minimum(low, high)
    step = (order + 1) // 2
    beside = z + step * (2 * (order % 2) - 1)
    beyond = jnp.where(high > low, order, nz - 1 - order)
    return jnp.where(order <= paired, beside, beyond)


def fused_kernel(
    nz,
    segments,
    experts,
    entering_ref,
    fresh_ref,
    mask_ref,
    router_ref,
    gain_ref,
    gate_hbm,
    up_hbm,
    down_hbm,
    out_ref,
    tokens,
    parts,
    core_in,
    y_in,
    z_in,
    x_in,
    hidden,
    gate_w,
    up_w,
    down_w,
    w_sem,
    za_s,
    za_r,
    ya_s,
    ya_r,
    ca_s,
    ca_r,
    cp_s,
    cp_r,
    yp_s,
    yp_r,
    zp_s,
    zp_r,
    x_s,
    x_r,
):
    micro, rows, width = out_ref.shape
    hid = gate_w.shape[1]
    seg, e, c = lax.axis_index("segment"), lax.axis_index("expert"), lax.axis_index("dp")
    z, y = e // 2, e % 2
    expert_id = 2 * e + c
    tile = 256

    def at(start, size):
        return pl.ds(pl.multiple_of(start, rows), size)

    half = c * 2 * rows
    own = at(half + y * rows, rows)
    other = at(half + (1 - y) * rows, rows)
    sibling = (seg, e, 1 - c)
    across = (seg, 2 * z + 1 - y, c)

    def line(direction):
        return (seg, e + 2 * (1 - 2 * direction), c)

    def remote(src, dst, send, recv, target):
        return pltpu.make_async_remote_copy(
            src_ref=src,
            dst_ref=dst,
            send_sem=send,
            recv_sem=recv,
            device_id=target,
            device_id_type=MESH,
        )

    def z_tokens(p, t, k):
        block = tokens.at[p, t, own]
        return remote(block, block, za_s.at[p, k, t], za_r.at[p, k, t], line(k))

    def y_tokens(p, t):
        block = tokens.at[p, t, own]
        return remote(block, block, ya_s.at[p, t], ya_r.at[p, t], across)

    def c_tokens(p, t, yy):
        block = tokens.at[p, t, at(half + yy * rows, rows)]
        return remote(block, block, ca_s.at[p, t, yy], ca_r.at[p, t, yy], sibling)

    def c_parts(p, t):
        src = parts.at[p, t, at((1 - c) * 2 * rows, 2 * rows)]
        return remote(src, core_in.at[p, t], cp_s.at[p, t], cp_r.at[p, t], sibling)

    def y_parts(p, t):
        return remote(parts.at[p, t, other], y_in.at[p, t], yp_s.at[p, t], yp_r.at[p, t], across)

    def z_parts(p, t, k):
        return remote(
            parts.at[p, t, own], z_in.at[p, k, t], zp_s.at[p, k, t], zp_r.at[p, k, t], line(k)
        )

    def x_out(p):
        return remote(out_ref.at[p], x_in.at[p], x_s.at[p], x_r.at[p], (seg + 1, e, c))

    loads = [
        pltpu.make_async_copy(src.at[0, 0], dst, w_sem.at[n])
        for n, (src, dst) in enumerate(((gate_hbm, gate_w), (up_hbm, up_w), (down_hbm, down_w)))
    ]
    for load in loads:
        load.start()

    barrier = pltpu.get_barrier_semaphore()

    def greet(target):
        pl.semaphore_signal(barrier, inc=1, device_id=target, device_id_type=MESH)

    greet(sibling)
    greet(across)
    for present, target in (
        (z < nz - 1, line(0)),
        (z > 0, line(1)),
        (seg < segments - 1, (seg + 1, e, c)),
        (seg > 0, (seg - 1, e, c)),
    ):
        pl.when(present)(functools.partial(greet, target))
    peers = 2
    for places in (z, nz - 1 - z, seg, segments - 1 - seg):
        peers = peers + jnp.minimum(places, 1)
    pl.semaphore_wait(barrier, peers)

    lanes = lax.broadcasted_iota(jnp.int32, (rows, LANES), 1)
    plane_lanes = lax.broadcasted_iota(jnp.int32, (4 * rows, LANES), 1)

    def normalise(p, source):
        values = source[...].astype(jnp.float32)
        inv_scale = lax.rsqrt(jnp.mean(values * values, axis=1, keepdims=True) + 1e-06)
        normed = (values * inv_scale * gain_ref[...]).astype(jnp.bfloat16)
        tokens[p, z, own, :width] = normed
        logits = jnp.dot(normed, router_ref[...], preferred_element_type=jnp.float32)
        scores = jnp.where(mask_ref[p] > 0.0, 1.0 / (1.0 + jnp.exp(-logits)), 0.0)
        total = jnp.sum(jnp.where(lanes < experts, scores, 0.0), axis=1, keepdims=True)
        mixing = scores / total
        rounded = mixing.astype(jnp.bfloat16).astype(jnp.float32)
        coded = jnp.where(lanes < experts, rounded, mixing - rounded)
        tokens[p, z, own, width:] = coded.astype(jnp.bfloat16)

    def acquire(p, t):
        @pl.when(t < z)
        def _():
            z_tokens(p, t, 0).wait_recv()

        @pl.when(t > z)
        def _():
            z_tokens(p, t, 1).wait_recv()

        @pl.when((t <= z) & (z < nz - 1))
        def _():
            z_tokens(p, t, 0).start()

        @pl.when((t >= z) & (z > 0))
        def _():
            z_tokens(p, t, 1).start()

        y_tokens(p, t).start()
        c_tokens(p, t, y).start()

    def finish(p, t, between):
        y_tokens(p, t).wait_recv()
        c_tokens(p, t, 1 - y).start()
        between()
        c_tokens(p, t, 0).wait_recv()
        c_tokens(p, t, 1).wait_recv()
        coded = tokens[p, t, :, width:].astype(jnp.float32)
        mine = (plane_lanes == expert_id) | (plane_lanes == expert_id + experts)
        weight = jnp.sum(jnp.where(mine, coded, 0.0), axis=1, keepdims=True)

        @pl.loop(0, hid // tile)
        def _(n):
            columns = pl.ds(pl.multiple_of(n * tile, tile), tile)
            block = tokens[p, t, :, :width]
            gate = jnp.dot(block, gate_w[:, columns], preferred_element_type=jnp.float32)
            upper = jnp.dot(block, up_w[:, columns], preferred_element_type=jnp.float32)
            hidden[:, columns] = (gate / (1.0 + jnp.exp(-gate)) * upper).astype(jnp.bfloat16)

        @pl.loop(0, width // tile)
        def _(n):
            columns = pl.ds(pl.multiple_of(n * tile, tile), tile)
            projected = jnp.dot(
                hidden[...], down_w[:, columns], preferred_element_type=jnp.float32
            )
            parts[p, t, :, columns] = (projected * weight).astype(jnp.bfloat16)

        c_parts(p, t).start()

    def both_cores(p, t):
        c_parts(p, t).wait_recv()

        @pl.loop(0, 2 * rows // 16)
        def _(n):
            here = pl.ds(pl.multiple_of(half + n * 16, 16), 16)
            there = pl.ds(pl.multiple_of(n * 16, 16), 16)
            parts[p, t, here] = (
                parts[p, t, here].astype(jnp.float32) + core_in[p, t, there].astype(jnp.float32)
            ).astype(jnp.bfloat16)

        y_parts(p, t).start()

    def along_line(p, t):
        y_parts(p, t).wait_recv()

        def total(received):
            @pl.loop(0, rows // 16)
            def _(n):
                here = pl.ds(pl.multiple_of(half + y * rows + n * 16, 16), 16)
                there = pl.ds(pl.multiple_of(n * 16, 16), 16)
                value = parts[p, t, here].astype(jnp.float32)
                value = value + y_in[p, t, there].astype(jnp.float32)
                if received is not None:
                    value = value + z_in[p, received, t, there].astype(jnp.float32)
                parts[p, t, here] = value.astype(jnp.bfloat16)

        for k, beyond, outermost in ((0, t > z, z == 0), (1, t < z, z == nz - 1)):

            @pl.when(beyond & outermost)
            def _(k=k):
                total(None)
                z_parts(p, t, k).start()

            @pl.when(beyond & jnp.logical_not(outermost))
            def _(k=k):
                z_parts(p, t, k).wait_recv()
                total(k)
                z_parts(p, t, k).start()

    def complete(p, source):
        y_parts(p, z).wait_recv()
        pl.when(z > 0)(lambda: z_parts(p, z, 0).wait_recv())
        pl.when(z < nz - 1)(lambda: z_parts(p, z, 1).wait_recv())

        def add(received):
            @pl.loop(0, rows // 16)
            def _(n):
                here = pl.ds(pl.multiple_of(half + y * rows + n * 16, 16), 16)
                there = pl.ds(pl.multiple_of(n * 16, 16), 16)
                value = source[there].astype(jnp.float32)
                value = value + parts[p, z, here].astype(jnp.float32)
                value = value + y_in[p, z, there].astype(jnp.float32)
                for k in received:
                    value = value + z_in[p, k, z, there].astype(jnp.float32)
                out_ref[p, there] = value.astype(jnp.bfloat16)

        pl.when(z == 0)(lambda: add((1,)))
        pl.when(z == nz - 1)(lambda: add((0,)))
        pl.when((z > 0) & (z < nz - 1))(lambda: add((0, 1)))

    for p in range(micro):
        source = x_in.at[p]
        if p == 0:
            source = entering_ref
        else:

            @pl.when(seg == 0)
            def _(p=p):
                x_in[p] = fresh_ref[p - 1]

            @pl.when(seg > 0)
            def _(p=p):
                x_out(p - 1).wait_recv()
                x_in[p] = x_in[p - 1]

        normalise(p, source)
        acquire(p, z)

        @pl.loop(1, nz)
        def _(order, p=p):
            acquire(p, near_first(order, z, nz))
            if p == 0:

                @pl.when(order == 1)
                def _():
                    for load in loads:
                        load.wait()

            finish(p, near_first(order - 1, z, nz), lambda: None)

        finish(p, near_first(nz - 1, z, nz), lambda: both_cores(p, z))

        @pl.loop(1, nz)
        def _(back, p=p):
            both_cores(p, near_first(nz - back, z, nz))

        @pl.loop(1, nz)
        def _(back, p=p):
            along_line(p, near_first(nz - back, z, nz))

        complete(p, source)
        if p < micro - 1:

            @pl.when(seg < segments - 1)
            def _(p=p):
                x_out(p).start()

    for p in range(micro):

        @pl.loop(0, nz)
        def _(t, p=p):
            @pl.when((t <= z) & (z < nz - 1))
            def _():
                z_tokens(p, t, 0).wait_send()

            @pl.when((t >= z) & (z > 0))
            def _():
                z_tokens(p, t, 1).wait_send()

            y_tokens(p, t).wait_send()
            c_tokens(p, t, 0).wait_send()
            c_tokens(p, t, 1).wait_send()
            c_parts(p, t).wait_send()
            y_parts(p, t).wait_send()

            @pl.when(t > z)
            def _():
                z_parts(p, t, 0).wait_send()

            @pl.when(t < z)
            def _():
                z_parts(p, t, 1).wait_send()

        if p < micro - 1:

            @pl.when(seg < segments - 1)
            def _(p=p):
                x_out(p).wait_send()


def fused_shards(nz, entering, fresh, w_gate, w_up, w_down, router, gain, routes):
    micro, rows, top_count = routes.shape[1:]
    width, experts = router.shape[1:]
    hid = w_gate.shape[3]
    segments = lax.axis_size("segment")
    ids = jnp.arange(LANES, dtype=jnp.int32)
    ids = jnp.where(ids < 2 * experts, ids % experts, -1)
    mask = jnp.any(routes[0][:, :, :, None] == ids[None, None, None, :], axis=2)
    spare = jnp.zeros((width, LANES - 2 * experts), jnp.bfloat16)
    doubled = jnp.concatenate([router[0], router[0], spare], axis=1)
    bf16 = jnp.bfloat16
    vmem = pl.BlockSpec(memory_space=pltpu.VMEM)
    hbm = pl.BlockSpec(memory_space=pl.ANY)
    sem = pltpu.SemaphoreType.DMA
    out = pl.pallas_call(
        functools.partial(fused_kernel, nz, segments, experts),
        out_shape=jax.ShapeDtypeStruct((micro, rows, width), bf16),
        in_specs=[vmem] * 5 + [hbm] * 3,
        out_specs=vmem,
        scratch_shapes=[
            pltpu.VMEM((micro, nz, 4 * rows, width + LANES), bf16),
            pltpu.VMEM((micro, nz, 4 * rows, width), bf16),
            pltpu.VMEM((micro, nz, 2 * rows, width), bf16),
            pltpu.VMEM((micro, nz, rows, width), bf16),
            pltpu.VMEM((micro, 2, nz, rows, width), bf16),
            pltpu.VMEM((micro, rows, width), bf16),
            pltpu.VMEM((4 * rows, hid), bf16),
            pltpu.VMEM((width, hid), bf16),
            pltpu.VMEM((width, hid), bf16),
            pltpu.VMEM((hid, width), bf16),
            sem((3,)),
        ]
        + [sem((micro, 2, nz))] * 2
        + [sem((micro, nz))] * 2
        + [sem((micro, nz, 2))] * 2
        + [sem((micro, nz))] * 4
        + [sem((micro, 2, nz))] * 2
        + [sem((micro,))] * 2,
        compiler_params=pltpu.CompilerParams(
            collective_id=0, has_side_effects=True, vmem_limit_bytes=60 * 1024 * 1024
        ),
        cost_estimate=pl.CostEstimate(
            flops=6 * micro * nz * 4 * rows * width * hid,
            bytes_accessed=6 * width * hid,
            transcendentals=micro * nz * 4 * rows * hid,
        ),
    )(entering[0], fresh, mask.astype(jnp.float32), doubled, gain, w_gate, w_up, w_down)
    return out[None]


def solution(mesh):
    in_specs = (
        P("segment", ("expert", "dp"), None),
        P(None, ("expert", "dp"), None),
        P("segment", ("expert", "dp"), None, None),
        P("segment", ("expert", "dp"), None, None),
        P("segment", ("expert", "dp"), None, None),
        P("segment", None, None),
        P("segment", None),
        P("segment", None, ("expert", "dp"), None),
    )
    out_specs = P("segment", None, ("expert", "dp"), None)
    positions = {getattr(device, "coords", (0, 0, 0))[1] for device in mesh.devices.flat}
    line = mesh.shape["expert"] // 2
    body = shards
    if len(positions) == 2 and mesh.shape["dp"] == 2 and 2 <= line <= 4:
        body = functools.partial(fused_shards, line)
    return jax.shard_map(body, mesh=mesh, in_specs=in_specs, out_specs=out_specs, check_vma=False)
```

```python
import functools

import jax
import jax.numpy as jnp
from jax import lax
from jax.experimental import pallas as pl
from jax.experimental.pallas import tpu as pltpu
from jax.sharding import PartitionSpec as P


def shifted(value, axis, steps):
    count = lax.axis_size(axis)
    leading, last = (max(0, -steps), min(count, count - steps))
    return lax.ppermute(value, axis, [(source, source + steps) for source in range(leading, last)])


def expert_rows(slot_rows, gate_weight, up_weight, down_weight):
    model_width = slot_rows.shape[-1]
    flattened = slot_rows.reshape(-1, model_width)
    gate_out = jnp.dot(flattened, gate_weight, preferred_element_type=jnp.float32)
    upper = jnp.dot(flattened, up_weight, preferred_element_type=jnp.float32)
    hidden = (jax.nn.silu(gate_out) * upper).astype(jnp.bfloat16)
    projected = jnp.dot(hidden, down_weight, preferred_element_type=jnp.float32).astype(
        jnp.bfloat16
    )
    return projected.reshape(slot_rows.shape)


def routed_slots(chosen_ids, expert_count):
    onehot = (chosen_ids[:, None] == jnp.arange(expert_count, dtype=jnp.int32)[None, :]).astype(
        jnp.int32
    )
    before = jnp.cumsum(onehot, axis=0) - onehot
    return jnp.sum(before * onehot, axis=1)


def section(incoming, gate_weight, up_weight, down_weight, router_layer, gain_layer, chosen_ids):
    tok_rows, model_width = incoming.shape
    top_count = chosen_ids.shape[1]
    experts = router_layer.shape[1]
    capacity = 4 * tok_rows * top_count // (3 * experts)
    values = incoming.astype(jnp.float32)
    inv_scale = lax.rsqrt(jnp.mean(values * values, axis=1, keepdims=True) + 1e-06)
    normed = (values * inv_scale * gain_layer[None, :]).astype(jnp.bfloat16)
    logits = jnp.dot(normed, router_layer, preferred_element_type=jnp.float32)
    scores = jax.nn.sigmoid(logits)
    chosen = jnp.take_along_axis(scores, chosen_ids, axis=1)
    mixing = chosen / jnp.sum(chosen, axis=1, keepdims=True)
    flat_picks = chosen_ids.reshape(-1)
    slot_ids = routed_slots(flat_picks, experts)
    owners = jnp.arange(tok_rows * top_count, dtype=jnp.int32) // top_count
    source = jnp.full((experts, capacity), tok_rows, jnp.int32).at[flat_picks, slot_ids].set(owners)
    padded = jnp.concatenate([normed, jnp.zeros((1, model_width), jnp.bfloat16)], axis=0)
    outgoing = padded[source]
    processed = expert_rows(
        lax.all_to_all(outgoing, ("expert", "dp"), split_axis=0, concat_axis=0, tiled=True),
        gate_weight,
        up_weight,
        down_weight,
    )
    returned = lax.all_to_all(processed, ("expert", "dp"), split_axis=0, concat_axis=0, tiled=True)
    landed = returned[flat_picks, slot_ids].reshape(tok_rows, top_count, model_width)
    summed = values + jnp.sum(landed.astype(jnp.float32) * mixing[:, :, None], axis=1)
    return summed.astype(jnp.bfloat16)


def shards(entering, fresh, w_gate, w_up, w_down, router, gain, routes):
    segment_id = lax.axis_index("segment")
    micro_count = routes.shape[1]
    current = entering[0]
    results = []
    for step_index in range(micro_count):
        if step_index > 0:
            arrived = shifted(results[-1], "segment", 1)
            current = jnp.where(segment_id == 0, fresh[step_index - 1], arrived)
        output = section(
            current,
            w_gate[0, 0],
            w_up[0, 0],
            w_down[0, 0],
            router[0],
            gain[0],
            routes[0, step_index],
        )
        results.append(output)
    return jnp.stack(results)[None]


LANES = 128
MESH = pl.DeviceIdType.MESH


def near_first(order, z, nz):
    low, high = z, nz - 1 - z
    paired = 2 * jnp.minimum(low, high)
    step = (order + 1) // 2
    beside = z + step * (2 * (order % 2) - 1)
    beyond = jnp.where(high > low, order, nz - 1 - order)
    return jnp.where(order <= paired, beside, beyond)


def fused_kernel(
    nz,
    segments,
    experts,
    entering_ref,
    fresh_ref,
    routes_ref,
    router_ref,
    gain_ref,
    gate_hbm,
    up_hbm,
    down_hbm,
    out_ref,
    tokens,
    parts,
    core_in,
    y_in,
    z_in,
    x_in,
    hidden,
    router_w,
    gate_w,
    up_w,
    down_w,
    w_sem,
    za_s,
    za_r,
    ya_s,
    ya_r,
    ca_s,
    ca_r,
    cp_s,
    cp_r,
    yp_s,
    yp_r,
    zp_s,
    zp_r,
    x_s,
    x_r,
):
    micro, rows, width = out_ref.shape
    hid = gate_w.shape[1]
    seg, e, c = lax.axis_index("segment"), lax.axis_index("expert"), lax.axis_index("dp")
    z, y = e // 2, e % 2
    expert_id = 2 * e + c
    tile = 256

    def at(start, size):
        return pl.ds(pl.multiple_of(start, rows), size)

    half = c * 2 * rows
    own = at(half + y * rows, rows)
    other = at(half + (1 - y) * rows, rows)
    sibling = (seg, e, 1 - c)
    across = (seg, 2 * z + 1 - y, c)

    def line(direction):
        return (seg, e + 2 * (1 - 2 * direction), c)

    def remote(src, dst, send, recv, target):
        return pltpu.make_async_remote_copy(
            src_ref=src,
            dst_ref=dst,
            send_sem=send,
            recv_sem=recv,
            device_id=target,
            device_id_type=MESH,
        )

    def z_tokens(p, t, k):
        block = tokens.at[p, t, own]
        return remote(block, block, za_s.at[p, k, t], za_r.at[p, k, t], line(k))

    def y_tokens(p, t):
        block = tokens.at[p, t, own]
        return remote(block, block, ya_s.at[p, t], ya_r.at[p, t], across)

    def c_tokens(p, t, yy):
        block = tokens.at[p, t, at(half + yy * rows, rows)]
        return remote(block, block, ca_s.at[p, t, yy], ca_r.at[p, t, yy], sibling)

    def c_parts(p, t):
        src = parts.at[p, t, at((1 - c) * 2 * rows, 2 * rows)]
        return remote(src, core_in.at[p, t], cp_s.at[p, t], cp_r.at[p, t], sibling)

    def y_parts(p, t):
        return remote(parts.at[p, t, other], y_in.at[p, t], yp_s.at[p, t], yp_r.at[p, t], across)

    def z_parts(p, t, k):
        return remote(
            parts.at[p, t, own], z_in.at[p, k, t], zp_s.at[p, k, t], zp_r.at[p, k, t], line(k)
        )

    def x_out(p):
        return remote(out_ref.at[p], x_in.at[p], x_s.at[p], x_r.at[p], (seg + 1, e, c))

    router_w[...] = jnp.zeros_like(router_w)
    router_w[:experts] = router_ref[...]
    router_w[experts : 2 * experts] = router_ref[...]
    loads = [
        pltpu.make_async_copy(src.at[0, 0], dst, w_sem.at[n])
        for n, (src, dst) in enumerate(((gate_hbm, gate_w), (up_hbm, up_w), (down_hbm, down_w)))
    ]
    for load in loads:
        load.start()

    barrier = pltpu.get_barrier_semaphore()

    def greet(target):
        pl.semaphore_signal(barrier, inc=1, device_id=target, device_id_type=MESH)

    greet(sibling)
    greet(across)
    for present, target in (
        (z < nz - 1, line(0)),
        (z > 0, line(1)),
        (seg < segments - 1, (seg + 1, e, c)),
        (seg > 0, (seg - 1, e, c)),
    ):
        pl.when(present)(functools.partial(greet, target))
    peers = 2
    for places in (z, nz - 1 - z, seg, segments - 1 - seg):
        peers = peers + jnp.minimum(places, 1)
    pl.semaphore_wait(barrier, peers)

    lanes = lax.broadcasted_iota(jnp.int32, (rows, LANES), 1)
    plane_lanes = lax.broadcasted_iota(jnp.int32, (4 * rows, LANES), 1)

    def normalise(p, source):
        values = source[...].astype(jnp.float32)
        inv_scale = lax.rsqrt(jnp.mean(values * values, axis=1, keepdims=True) + 1e-06)
        normed = (values * inv_scale * gain_ref[...]).astype(jnp.bfloat16)
        tokens[p, z, own, :width] = normed
        logits = lax.dot_general(
            normed,
            router_w[...],
            (((1,), (1,)), ((), ())),
            preferred_element_type=jnp.float32,
        )
        chosen = routes_ref[p]
        ids = jnp.where(lanes < experts, lanes, lanes - experts)
        named = chosen[:, :1] == ids
        for n in range(1, chosen.shape[1]):
            named = named | (chosen[:, n : n + 1] == ids)
        scores = jnp.where(named, 1.0 / (1.0 + jnp.exp(-logits)), 0.0)
        total = jnp.sum(jnp.where(lanes < experts, scores, 0.0), axis=1, keepdims=True)
        mixing = scores / total
        rounded = mixing.astype(jnp.bfloat16).astype(jnp.float32)
        coded = jnp.where(lanes < experts, rounded, mixing - rounded)
        tokens[p, z, own, width:] = coded.astype(jnp.bfloat16)

    def acquire(p, t):
        @pl.when(t < z)
        def _():
            z_tokens(p, t, 0).wait_recv()

        @pl.when(t > z)
        def _():
            z_tokens(p, t, 1).wait_recv()

        @pl.when((t <= z) & (z < nz - 1))
        def _():
            z_tokens(p, t, 0).start()

        @pl.when((t >= z) & (z > 0))
        def _():
            z_tokens(p, t, 1).start()

        y_tokens(p, t).start()
        c_tokens(p, t, y).start()

    def finish(p, t, between):
        y_tokens(p, t).wait_recv()
        c_tokens(p, t, 1 - y).start()
        between()
        c_tokens(p, t, 0).wait_recv()
        c_tokens(p, t, 1).wait_recv()
        coded = tokens[p, t, :, width:].astype(jnp.float32)
        mine = (plane_lanes == expert_id) | (plane_lanes == expert_id + experts)
        weight = jnp.sum(jnp.where(mine, coded, 0.0), axis=1, keepdims=True)

        @pl.loop(0, hid // tile)
        def _(n):
            columns = pl.ds(pl.multiple_of(n * tile, tile), tile)
            block = tokens[p, t, :, :width]
            gate = jnp.dot(block, gate_w[:, columns], preferred_element_type=jnp.float32)
            upper = jnp.dot(block, up_w[:, columns], preferred_element_type=jnp.float32)
            hidden[:, columns] = (gate / (1.0 + jnp.exp(-gate)) * upper).astype(jnp.bfloat16)

        @pl.loop(0, width // tile)
        def _(n):
            columns = pl.ds(pl.multiple_of(n * tile, tile), tile)
            projected = jnp.dot(
                hidden[...], down_w[:, columns], preferred_element_type=jnp.float32
            )
            parts[p, t, :, columns] = (projected * weight).astype(jnp.bfloat16)

        c_parts(p, t).start()

    def both_cores(p, t):
        c_parts(p, t).wait_recv()

        @pl.loop(0, 2 * rows // 16)
        def _(n):
            here = pl.ds(pl.multiple_of(half + n * 16, 16), 16)
            there = pl.ds(pl.multiple_of(n * 16, 16), 16)
            parts[p, t, here] = (
                parts[p, t, here].astype(jnp.float32) + core_in[p, t, there].astype(jnp.float32)
            ).astype(jnp.bfloat16)

    def along_line(p, t):
        def total(received):
            @pl.loop(0, rows // 16)
            def _(n):
                here = pl.ds(pl.multiple_of(half + y * rows + n * 16, 16), 16)
                there = pl.ds(pl.multiple_of(n * 16, 16), 16)
                value = parts[p, t, here].astype(jnp.float32)
                value = value + y_in[p, t, there].astype(jnp.float32)
                if received is not None:
                    value = value + z_in[p, received, t, there].astype(jnp.float32)
                parts[p, t, here] = value.astype(jnp.bfloat16)

        for k, beyond, outermost in ((0, t > z, z == 0), (1, t < z, z == nz - 1)):

            @pl.when(beyond & outermost)
            def _(k=k):
                total(None)
                z_parts(p, t, k).start()

            @pl.when(beyond & jnp.logical_not(outermost))
            def _(k=k):
                z_parts(p, t, k).wait_recv()
                total(k)
                z_parts(p, t, k).start()

    def complete(p, source):
        y_parts(p, z).wait_recv()
        pl.when(z > 0)(lambda: z_parts(p, z, 0).wait_recv())
        pl.when(z < nz - 1)(lambda: z_parts(p, z, 1).wait_recv())

        def add(received):
            @pl.loop(0, rows // 16)
            def _(n):
                here = pl.ds(pl.multiple_of(half + y * rows + n * 16, 16), 16)
                there = pl.ds(pl.multiple_of(n * 16, 16), 16)
                value = source[there].astype(jnp.float32)
                value = value + parts[p, z, here].astype(jnp.float32)
                value = value + y_in[p, z, there].astype(jnp.float32)
                for k in received:
                    value = value + z_in[p, k, z, there].astype(jnp.float32)
                out_ref[p, there] = value.astype(jnp.bfloat16)

        pl.when(z == 0)(lambda: add((1,)))
        pl.when(z == nz - 1)(lambda: add((0,)))
        pl.when((z > 0) & (z < nz - 1))(lambda: add((0, 1)))

    for p in range(micro):
        source = x_in.at[p]
        if p == 0:
            source = entering_ref
        else:

            @pl.when(seg == 0)
            def _(p=p):
                x_in[p] = fresh_ref[p - 1]

            @pl.when(seg > 0)
            def _(p=p):
                x_out(p - 1).wait_recv()
                x_in[p] = x_in[p - 1]

        normalise(p, source)
        acquire(p, z)

        @pl.loop(1, nz)
        def _(distance, p=p):
            pl.when(z + distance < nz)(lambda: acquire(p, z + distance))
            pl.when(z >= distance)(lambda: acquire(p, z - distance))
            if p == 0:

                @pl.when(distance == 1)
                def _():
                    for load in loads:
                        load.wait()

            finish(p, near_first(distance - 1, z, nz), lambda: None)

        def own_plane(p=p):
            both_cores(p, z)
            y_parts(p, z).start()

        farthest = near_first(nz - 1, z, nz)
        finish(p, farthest, own_plane)
        both_cores(p, farthest)
        y_parts(p, farthest).start()

        @pl.loop(1, nz)
        def _(back, p=p):
            t = near_first(nz - back, z, nz)
            following = near_first(nz - back - 1, z, nz)
            more = back < nz - 1
            pl.when(more)(lambda: both_cores(p, following))
            y_parts(p, t).wait_recv()
            pl.when(more)(lambda: y_parts(p, following).start())
            along_line(p, t)

        complete(p, source)
        if p < micro - 1:

            @pl.when(seg < segments - 1)
            def _(p=p):
                x_out(p).start()

    for p in range(micro):

        @pl.loop(0, nz)
        def _(t, p=p):
            @pl.when((t <= z) & (z < nz - 1))
            def _():
                z_tokens(p, t, 0).wait_send()

            @pl.when((t >= z) & (z > 0))
            def _():
                z_tokens(p, t, 1).wait_send()

            y_tokens(p, t).wait_send()
            c_tokens(p, t, 0).wait_send()
            c_tokens(p, t, 1).wait_send()
            c_parts(p, t).wait_send()
            y_parts(p, t).wait_send()

            @pl.when(t > z)
            def _():
                z_parts(p, t, 0).wait_send()

            @pl.when(t < z)
            def _():
                z_parts(p, t, 1).wait_send()

        if p < micro - 1:

            @pl.when(seg < segments - 1)
            def _(p=p):
                x_out(p).wait_send()


def fused_shards(nz, entering, fresh, w_gate, w_up, w_down, router, gain, routes):
    micro, rows, top_count = routes.shape[1:]
    width, experts = router.shape[1:]
    hid = w_gate.shape[3]
    segments = lax.axis_size("segment")
    bf16 = jnp.bfloat16
    vmem = pl.BlockSpec(memory_space=pltpu.VMEM)
    hbm = pl.BlockSpec(memory_space=pl.ANY)
    sem = pltpu.SemaphoreType.DMA
    out = pl.pallas_call(
        functools.partial(fused_kernel, nz, segments, experts),
        out_shape=jax.ShapeDtypeStruct((micro, rows, width), bf16),
        in_specs=[vmem] * 5 + [hbm] * 3,
        out_specs=vmem,
        scratch_shapes=[
            pltpu.VMEM((micro, nz, 4 * rows, width + LANES), bf16),
            pltpu.VMEM((micro, nz, 4 * rows, width), bf16),
            pltpu.VMEM((micro, nz, 2 * rows, width), bf16),
            pltpu.VMEM((micro, nz, rows, width), bf16),
            pltpu.VMEM((micro, 2, nz, rows, width), bf16),
            pltpu.VMEM((micro, rows, width), bf16),
            pltpu.VMEM((4 * rows, hid), bf16),
            pltpu.VMEM((LANES, width), bf16),
            pltpu.VMEM((width, hid), bf16),
            pltpu.VMEM((width, hid), bf16),
            pltpu.VMEM((hid, width), bf16),
            sem((3,)),
        ]
        + [sem((micro, 2, nz))] * 2
        + [sem((micro, nz))] * 2
        + [sem((micro, nz, 2))] * 2
        + [sem((micro, nz))] * 4
        + [sem((micro, 2, nz))] * 2
        + [sem((micro,))] * 2,
        compiler_params=pltpu.CompilerParams(
            collective_id=0, has_side_effects=True, vmem_limit_bytes=60 * 1024 * 1024
        ),
        cost_estimate=pl.CostEstimate(
            flops=6 * micro * nz * 4 * rows * width * hid,
            bytes_accessed=6 * width * hid,
            transcendentals=micro * nz * 4 * rows * hid,
        ),
    )(entering[0], fresh, routes[0], router[0].T, gain, w_gate, w_up, w_down)
    return out[None]


def solution(mesh):
    in_specs = (
        P("segment", ("expert", "dp"), None),
        P(None, ("expert", "dp"), None),
        P("segment", ("expert", "dp"), None, None),
        P("segment", ("expert", "dp"), None, None),
        P("segment", ("expert", "dp"), None, None),
        P("segment", None, None),
        P("segment", None),
        P("segment", None, ("expert", "dp"), None),
    )
    out_specs = P("segment", None, ("expert", "dp"), None)
    positions = {getattr(device, "coords", (0, 0, 0))[1] for device in mesh.devices.flat}
    line = mesh.shape["expert"] // 2
    body = shards
    if len(positions) == 2 and mesh.shape["dp"] == 2 and 2 <= line <= 4:
        body = functools.partial(fused_shards, line)
    return jax.shard_map(body, mesh=mesh, in_specs=in_specs, out_specs=out_specs, check_vma=False)
```

```python
import functools

import jax
import jax.numpy as jnp
from jax import lax
from jax.experimental import pallas as pl
from jax.experimental.pallas import tpu as pltpu
from jax.sharding import PartitionSpec as P


def shifted(value, axis, steps):
    count = lax.axis_size(axis)
    leading, last = (max(0, -steps), min(count, count - steps))
    return lax.ppermute(value, axis, [(source, source + steps) for source in range(leading, last)])


def expert_rows(slot_rows, gate_weight, up_weight, down_weight):
    model_width = slot_rows.shape[-1]
    flattened = slot_rows.reshape(-1, model_width)
    gate_out = jnp.dot(flattened, gate_weight, preferred_element_type=jnp.float32)
    upper = jnp.dot(flattened, up_weight, preferred_element_type=jnp.float32)
    hidden = (jax.nn.silu(gate_out) * upper).astype(jnp.bfloat16)
    projected = jnp.dot(hidden, down_weight, preferred_element_type=jnp.float32).astype(
        jnp.bfloat16
    )
    return projected.reshape(slot_rows.shape)


def routed_slots(chosen_ids, expert_count):
    onehot = (chosen_ids[:, None] == jnp.arange(expert_count, dtype=jnp.int32)[None, :]).astype(
        jnp.int32
    )
    before = jnp.cumsum(onehot, axis=0) - onehot
    return jnp.sum(before * onehot, axis=1)


def section(incoming, gate_weight, up_weight, down_weight, router_layer, gain_layer, chosen_ids):
    tok_rows, model_width = incoming.shape
    top_count = chosen_ids.shape[1]
    experts = router_layer.shape[1]
    capacity = 4 * tok_rows * top_count // (3 * experts)
    values = incoming.astype(jnp.float32)
    inv_scale = lax.rsqrt(jnp.mean(values * values, axis=1, keepdims=True) + 1e-06)
    normed = (values * inv_scale * gain_layer[None, :]).astype(jnp.bfloat16)
    logits = jnp.dot(normed, router_layer, preferred_element_type=jnp.float32)
    scores = jax.nn.sigmoid(logits)
    chosen = jnp.take_along_axis(scores, chosen_ids, axis=1)
    mixing = chosen / jnp.sum(chosen, axis=1, keepdims=True)
    flat_picks = chosen_ids.reshape(-1)
    slot_ids = routed_slots(flat_picks, experts)
    owners = jnp.arange(tok_rows * top_count, dtype=jnp.int32) // top_count
    source = jnp.full((experts, capacity), tok_rows, jnp.int32).at[flat_picks, slot_ids].set(owners)
    padded = jnp.concatenate([normed, jnp.zeros((1, model_width), jnp.bfloat16)], axis=0)
    outgoing = padded[source]
    processed = expert_rows(
        lax.all_to_all(outgoing, ("expert", "dp"), split_axis=0, concat_axis=0, tiled=True),
        gate_weight,
        up_weight,
        down_weight,
    )
    returned = lax.all_to_all(processed, ("expert", "dp"), split_axis=0, concat_axis=0, tiled=True)
    landed = returned[flat_picks, slot_ids].reshape(tok_rows, top_count, model_width)
    summed = values + jnp.sum(landed.astype(jnp.float32) * mixing[:, :, None], axis=1)
    return summed.astype(jnp.bfloat16)


def shards(entering, fresh, w_gate, w_up, w_down, router, gain, routes):
    segment_id = lax.axis_index("segment")
    micro_count = routes.shape[1]
    current = entering[0]
    results = []
    for step_index in range(micro_count):
        if step_index > 0:
            arrived = shifted(results[-1], "segment", 1)
            current = jnp.where(segment_id == 0, fresh[step_index - 1], arrived)
        output = section(
            current,
            w_gate[0, 0],
            w_up[0, 0],
            w_down[0, 0],
            router[0],
            gain[0],
            routes[0, step_index],
        )
        results.append(output)
    return jnp.stack(results)[None]


LANES = 128
MESH = pl.DeviceIdType.MESH


def near_first(order, z, nz):
    low, high = z, nz - 1 - z
    paired = 2 * jnp.minimum(low, high)
    step = (order + 1) // 2
    beside = z + step * (2 * (order % 2) - 1)
    beyond = jnp.where(high > low, order, nz - 1 - order)
    return jnp.where(order <= paired, beside, beyond)


def fused_kernel(
    nz,
    segments,
    experts,
    entering_ref,
    fresh_ref,
    routes_ref,
    router_ref,
    gain_ref,
    gate_hbm,
    up_hbm,
    down_hbm,
    out_ref,
    tokens,
    parts,
    core_in,
    y_in,
    z_in,
    x_in,
    hidden,
    router_w,
    gate_w,
    up_w,
    down_w,
    w_sem,
    za_s,
    za_r,
    ya_s,
    ya_r,
    ca_s,
    ca_r,
    cp_s,
    cp_r,
    yp_s,
    yp_r,
    zp_s,
    zp_r,
    x_s,
    x_r,
):
    micro, rows, width = out_ref.shape
    hid = gate_w.shape[1]
    seg, e, c = lax.axis_index("segment"), lax.axis_index("expert"), lax.axis_index("dp")
    z, y = e // 2, e % 2
    expert_id = 2 * e + c
    tile = 256

    def at(start, size):
        return pl.ds(pl.multiple_of(start, rows), size)

    half = c * 2 * rows
    own = at(half + y * rows, rows)
    other = at(half + (1 - y) * rows, rows)
    sibling = (seg, e, 1 - c)
    across = (seg, 2 * z + 1 - y, c)

    def line(direction):
        return (seg, e + 2 * (1 - 2 * direction), c)

    def remote(src, dst, send, recv, target):
        return pltpu.make_async_remote_copy(
            src_ref=src,
            dst_ref=dst,
            send_sem=send,
            recv_sem=recv,
            device_id=target,
            device_id_type=MESH,
        )

    def z_tokens(p, t, k):
        block = tokens.at[p, t, own]
        return remote(block, block, za_s.at[p, k, t], za_r.at[p, k, t], line(k))

    def y_tokens(p, t):
        block = tokens.at[p, t, own]
        return remote(block, block, ya_s.at[p, t], ya_r.at[p, t], across)

    def c_tokens(p, t, yy):
        block = tokens.at[p, t, at(half + yy * rows, rows)]
        return remote(block, block, ca_s.at[p, t, yy], ca_r.at[p, t, yy], sibling)

    def c_parts(p, t):
        src = parts.at[p, t, at((1 - c) * 2 * rows, 2 * rows)]
        return remote(src, core_in.at[p, t], cp_s.at[p, t], cp_r.at[p, t], sibling)

    def y_parts(p, t):
        return remote(parts.at[p, t, other], y_in.at[p, t], yp_s.at[p, t], yp_r.at[p, t], across)

    piece = rows // 2

    def z_parts(p, t, k, h):
        start = pl.multiple_of(half + y * rows + h * piece, piece)
        return remote(
            parts.at[p, t, pl.ds(start, piece)],
            z_in.at[p, k, t, pl.ds(h * piece, piece)],
            zp_s.at[p, k, t, h],
            zp_r.at[p, k, t, h],
            line(k),
        )

    def x_out(p):
        return remote(out_ref.at[p], x_in.at[p], x_s.at[p], x_r.at[p], (seg + 1, e, c))

    router_w[...] = jnp.zeros_like(router_w)
    router_w[:experts] = router_ref[...]
    router_w[experts : 2 * experts] = router_ref[...]
    loads = [
        pltpu.make_async_copy(src.at[0, 0], dst, w_sem.at[n])
        for n, (src, dst) in enumerate(((gate_hbm, gate_w), (up_hbm, up_w), (down_hbm, down_w)))
    ]
    for load in loads:
        load.start()

    barrier = pltpu.get_barrier_semaphore()

    def greet(target):
        pl.semaphore_signal(barrier, inc=1, device_id=target, device_id_type=MESH)

    greet(sibling)
    greet(across)
    for present, target in (
        (z < nz - 1, line(0)),
        (z > 0, line(1)),
        (seg < segments - 1, (seg + 1, e, c)),
        (seg > 0, (seg - 1, e, c)),
    ):
        pl.when(present)(functools.partial(greet, target))
    peers = 2
    for places in (z, nz - 1 - z, seg, segments - 1 - seg):
        peers = peers + jnp.minimum(places, 1)
    pl.semaphore_wait(barrier, peers)

    lanes = lax.broadcasted_iota(jnp.int32, (rows, LANES), 1)
    plane_lanes = lax.broadcasted_iota(jnp.int32, (4 * rows, LANES), 1)

    def normalise(p, source):
        values = source[...].astype(jnp.float32)
        inv_scale = lax.rsqrt(jnp.mean(values * values, axis=1, keepdims=True) + 1e-06)
        normed = (values * inv_scale * gain_ref[...]).astype(jnp.bfloat16)
        tokens[p, z, own, :width] = normed
        logits = lax.dot_general(
            normed,
            router_w[...],
            (((1,), (1,)), ((), ())),
            preferred_element_type=jnp.float32,
        )
        chosen = routes_ref[p]
        ids = jnp.where(lanes < experts, lanes, lanes - experts)
        named = chosen[:, :1] == ids
        for n in range(1, chosen.shape[1]):
            named = named | (chosen[:, n : n + 1] == ids)
        scores = jnp.where(named, 1.0 / (1.0 + jnp.exp(-logits)), 0.0)
        total = jnp.sum(jnp.where(lanes < experts, scores, 0.0), axis=1, keepdims=True)
        mixing = scores / total
        rounded = mixing.astype(jnp.bfloat16).astype(jnp.float32)
        coded = jnp.where(lanes < experts, rounded, mixing - rounded)
        tokens[p, z, own, width:] = coded.astype(jnp.bfloat16)

    def acquire(p, t):
        @pl.when(t < z)
        def _():
            z_tokens(p, t, 0).wait_recv()

        @pl.when(t > z)
        def _():
            z_tokens(p, t, 1).wait_recv()

        @pl.when((t <= z) & (z < nz - 1))
        def _():
            z_tokens(p, t, 0).start()

        @pl.when((t >= z) & (z > 0))
        def _():
            z_tokens(p, t, 1).start()

        y_tokens(p, t).start()
        c_tokens(p, t, y).start()

    def finish(p, t, between):
        y_tokens(p, t).wait_recv()
        c_tokens(p, t, 1 - y).start()
        between()
        c_tokens(p, t, 0).wait_recv()
        c_tokens(p, t, 1).wait_recv()
        coded = tokens[p, t, :, width:].astype(jnp.float32)
        mine = (plane_lanes == expert_id) | (plane_lanes == expert_id + experts)
        weight = jnp.sum(jnp.where(mine, coded, 0.0), axis=1, keepdims=True)

        @pl.loop(0, hid // tile)
        def _(n):
            columns = pl.ds(pl.multiple_of(n * tile, tile), tile)
            block = tokens[p, t, :, :width]
            gate = jnp.dot(block, gate_w[:, columns], preferred_element_type=jnp.float32)
            upper = jnp.dot(block, up_w[:, columns], preferred_element_type=jnp.float32)
            hidden[:, columns] = (gate / (1.0 + jnp.exp(-gate)) * upper).astype(jnp.bfloat16)

        @pl.loop(0, width // tile)
        def _(n):
            columns = pl.ds(pl.multiple_of(n * tile, tile), tile)
            projected = jnp.dot(
                hidden[...], down_w[:, columns], preferred_element_type=jnp.float32
            )
            parts[p, t, :, columns] = (projected * weight).astype(jnp.bfloat16)

        c_parts(p, t).start()

    def both_cores(p, t):
        c_parts(p, t).wait_recv()

        @pl.loop(0, 2 * rows // 16)
        def _(n):
            here = pl.ds(pl.multiple_of(half + n * 16, 16), 16)
            there = pl.ds(pl.multiple_of(n * 16, 16), 16)
            parts[p, t, here] = (
                parts[p, t, here].astype(jnp.float32) + core_in[p, t, there].astype(jnp.float32)
            ).astype(jnp.bfloat16)

    def along_line(p, t):
        def total(received, h):
            @pl.loop(h * piece // 16, (h + 1) * piece // 16)
            def _(n):
                here = pl.ds(pl.multiple_of(half + y * rows + n * 16, 16), 16)
                there = pl.ds(pl.multiple_of(n * 16, 16), 16)
                value = parts[p, t, here].astype(jnp.float32)
                value = value + y_in[p, t, there].astype(jnp.float32)
                if received is not None:
                    value = value + z_in[p, received, t, there].astype(jnp.float32)
                parts[p, t, here] = value.astype(jnp.bfloat16)

        for k, beyond, outermost in ((0, t > z, z == 0), (1, t < z, z == nz - 1)):

            @pl.when(beyond & outermost)
            def _(k=k):
                for h in range(2):
                    total(None, h)
                    z_parts(p, t, k, h).start()

            @pl.when(beyond & jnp.logical_not(outermost))
            def _(k=k):
                for h in range(2):
                    z_parts(p, t, k, h).wait_recv()
                    total(k, h)
                    z_parts(p, t, k, h).start()

    def complete(p, source):
        y_parts(p, z).wait_recv()
        for h in range(2):
            pl.when(z > 0)(lambda h=h: z_parts(p, z, 0, h).wait_recv())
            pl.when(z < nz - 1)(lambda h=h: z_parts(p, z, 1, h).wait_recv())

        def add(received):
            @pl.loop(0, rows // 16)
            def _(n):
                here = pl.ds(pl.multiple_of(half + y * rows + n * 16, 16), 16)
                there = pl.ds(pl.multiple_of(n * 16, 16), 16)
                value = source[there].astype(jnp.float32)
                value = value + parts[p, z, here].astype(jnp.float32)
                value = value + y_in[p, z, there].astype(jnp.float32)
                for k in received:
                    value = value + z_in[p, k, z, there].astype(jnp.float32)
                out_ref[p, there] = value.astype(jnp.bfloat16)

        pl.when(z == 0)(lambda: add((1,)))
        pl.when(z == nz - 1)(lambda: add((0,)))
        pl.when((z > 0) & (z < nz - 1))(lambda: add((0, 1)))

    for p in range(micro):
        source = x_in.at[p]
        if p == 0:
            source = entering_ref
        else:

            @pl.when(seg == 0)
            def _(p=p):
                x_in[p] = fresh_ref[p - 1]

            @pl.when(seg > 0)
            def _(p=p):
                x_out(p - 1).wait_recv()
                x_in[p] = x_in[p - 1]

        normalise(p, source)
        acquire(p, z)

        @pl.loop(1, nz)
        def _(distance, p=p):
            pl.when(z + distance < nz)(lambda: acquire(p, z + distance))
            pl.when(z >= distance)(lambda: acquire(p, z - distance))
            if p == 0:

                @pl.when(distance == 1)
                def _():
                    for load in loads:
                        load.wait()

            finish(p, near_first(distance - 1, z, nz), lambda: None)

        nearest = near_first(1, z, nz)
        outermost = (z == 0) | (z == nz - 1)

        def nearest_plane(p=p):
            both_cores(p, nearest)
            y_parts(p, nearest).start()

        farthest = near_first(nz - 1, z, nz)
        finish(p, farthest, nearest_plane)
        both_cores(p, farthest)
        y_parts(p, farthest).start()
        y_parts(p, nearest).wait_recv()
        pl.when(outermost)(lambda: along_line(p, nearest))

        @pl.loop(1, nz - 1)
        def _(back, p=p):
            t = near_first(nz - back, z, nz)
            order = nz - back - 1
            following = near_first(jnp.where(order > 1, order, 0), z, nz)
            both_cores(p, following)
            y_parts(p, t).wait_recv()
            y_parts(p, following).start()
            along_line(p, t)

        pl.when(jnp.logical_not(outermost))(lambda: along_line(p, nearest))
        complete(p, source)
        if p < micro - 1:

            @pl.when(seg < segments - 1)
            def _(p=p):
                x_out(p).start()

    for p in range(micro):

        @pl.loop(0, nz)
        def _(t, p=p):
            @pl.when((t <= z) & (z < nz - 1))
            def _():
                z_tokens(p, t, 0).wait_send()

            @pl.when((t >= z) & (z > 0))
            def _():
                z_tokens(p, t, 1).wait_send()

            y_tokens(p, t).wait_send()
            c_tokens(p, t, 0).wait_send()
            c_tokens(p, t, 1).wait_send()
            c_parts(p, t).wait_send()
            y_parts(p, t).wait_send()

            @pl.when(t > z)
            def _():
                for h in range(2):
                    z_parts(p, t, 0, h).wait_send()

            @pl.when(t < z)
            def _():
                for h in range(2):
                    z_parts(p, t, 1, h).wait_send()

        if p < micro - 1:

            @pl.when(seg < segments - 1)
            def _(p=p):
                x_out(p).wait_send()


def fused_shards(nz, entering, fresh, w_gate, w_up, w_down, router, gain, routes):
    micro, rows, top_count = routes.shape[1:]
    width, experts = router.shape[1:]
    hid = w_gate.shape[3]
    segments = lax.axis_size("segment")
    bf16 = jnp.bfloat16
    vmem = pl.BlockSpec(memory_space=pltpu.VMEM)
    hbm = pl.BlockSpec(memory_space=pl.ANY)
    sem = pltpu.SemaphoreType.DMA
    out = pl.pallas_call(
        functools.partial(fused_kernel, nz, segments, experts),
        out_shape=jax.ShapeDtypeStruct((micro, rows, width), bf16),
        in_specs=[vmem] * 5 + [hbm] * 3,
        out_specs=vmem,
        scratch_shapes=[
            pltpu.VMEM((micro, nz, 4 * rows, width + LANES), bf16),
            pltpu.VMEM((micro, nz, 4 * rows, width), bf16),
            pltpu.VMEM((micro, nz, 2 * rows, width), bf16),
            pltpu.VMEM((micro, nz, rows, width), bf16),
            pltpu.VMEM((micro, 2, nz, rows, width), bf16),
            pltpu.VMEM((micro, rows, width), bf16),
            pltpu.VMEM((4 * rows, hid), bf16),
            pltpu.VMEM((LANES, width), bf16),
            pltpu.VMEM((width, hid), bf16),
            pltpu.VMEM((width, hid), bf16),
            pltpu.VMEM((hid, width), bf16),
            sem((3,)),
        ]
        + [sem((micro, 2, nz))] * 2
        + [sem((micro, nz))] * 2
        + [sem((micro, nz, 2))] * 2
        + [sem((micro, nz))] * 4
        + [sem((micro, 2, nz, 2))] * 2
        + [sem((micro,))] * 2,
        compiler_params=pltpu.CompilerParams(
            collective_id=0, has_side_effects=True, vmem_limit_bytes=60 * 1024 * 1024
        ),
        cost_estimate=pl.CostEstimate(
            flops=6 * micro * nz * 4 * rows * width * hid,
            bytes_accessed=6 * width * hid,
            transcendentals=micro * nz * 4 * rows * hid,
        ),
    )(entering[0], fresh, routes[0], router[0].T, gain, w_gate, w_up, w_down)
    return out[None]


def solution(mesh):
    in_specs = (
        P("segment", ("expert", "dp"), None),
        P(None, ("expert", "dp"), None),
        P("segment", ("expert", "dp"), None, None),
        P("segment", ("expert", "dp"), None, None),
        P("segment", ("expert", "dp"), None, None),
        P("segment", None, None),
        P("segment", None),
        P("segment", None, ("expert", "dp"), None),
    )
    out_specs = P("segment", None, ("expert", "dp"), None)
    positions = {getattr(device, "coords", (0, 0, 0))[1] for device in mesh.devices.flat}
    line = mesh.shape["expert"] // 2
    body = shards
    if len(positions) == 2 and mesh.shape["dp"] == 2 and 3 <= line <= 4:
        body = functools.partial(fused_shards, line)
    return jax.shard_map(body, mesh=mesh, in_specs=in_specs, out_specs=out_specs, check_vma=False)
```
